256 devices in a mesh: grp: 2 (over x_hi), tp: 64 (over y, x_lo, z), seq: 2 (over core).
Axes of the slice: x: 4 (x_hi: 2, x_lo: 2; x = x_hi * 2 + x_lo), y: 4, z: 8, core: 2. Of those that a mesh axis runs over, the one named last changes fastest.
Arguments:
- feats: bfloat16 [256, 3, 8192], P('seq', None, 'tp'), may hold values from -6 to 6
- ids: int32 [256], replicated, may hold values from 0 to 16383
- loss_mask: int32 [256], replicated, may hold values 0 or 1
- owner: int32 [16, 1], replicated, may hold values from 0 to 1; in each aligned block of 8 rows (0 to 7, 8 to 15, ...) at most 6 rows name the same one
- shifts: int32 [3], replicated, may hold values from 0 to 15
- target_gain: bfloat16 [8192], replicated, may hold values from 0.5 to 1.5
- target_head: bfloat16 [8192, 16384], P(None, ('grp', 'tp')), may hold values from -16 to 16
- fc_weight: bfloat16 [24576, 8192], P('grp', 'tp'), may hold values from -0.0390625 to 0.0390625
- embed: bfloat16 [16384, 8192], P('grp', 'tp'), may hold values from -6 to 6
- draft_gain: bfloat16 [8192], replicated, may hold values from 0.5 to 1.5
- layer_weight: bfloat16 [8192, 8192], P(None, 'tp'), may hold values from -0.0625 to 0.0625
- draft_head: bfloat16 [8192, 16384], P(None, ('grp', 'tp')), may hold values from -16 to 16
Outputs:
- head_grad: bfloat16 [8192, 16384], P('seq', ('grp', 'tp'))
- slot_kl: float32 [3, 384], P(None, 'seq')
The draws below stay inside these ranges and needn't reach their ends.
Inputs may be any that keep to these rules, and one draw needn't show every extreme that they name: Among the blocks of one seq index (aligned blocks of 8 rows) no owner is named more than 6 times, a bound that some block reaches.
All inputs are finite; a program needn't handle non-finite values.
Results may differ from the reference program's by a relative error of at most 0.039.
The reference program's roundings to bfloat16 on the way count: a program that leaves them out, or rounds other values in their place, can miss the bound.
Values may be sent and summed in bfloat16 or wider, within the bound.
No kernel may reach another device: no remote copies, remote signals or barrier semaphores. Data moves between devices by JAX's collectives and lax.ppermute only.
A program may use at most 128 MiB of HBM per device.

```python
import math
import jax
import jax.numpy as jnp
import numpy as np
from jax import lax

D = 8192
BLK = 16
NBLK = 8
STEPS = 3
MOST = 6
TOKENS = 256
VOCAB = 16384
N_SEQ = 2


def head_values(key):
    first_key = jax.random.fold_in(key, 0)
    values = jax.random.normal(first_key, (D, VOCAB), jnp.float32) * (3.0 / math.sqrt(D))
    return jnp.clip(values, -16.0, 16.0).astype(jnp.bfloat16)


def draw_target_head(key, part):
    key = jax.random.fold_in(key, 11)
    return head_values(key)


def draw_draft_head(key, part):
    key = jax.random.fold_in(key, 23)
    return head_values(key)


def touch_ends(result, key, smallest, top_value):
    longest = result.shape.index(max(result.shape))
    spots = []
    for shift in (0, 1):
        where = [jax.random.randint(jax.random.fold_in(key, axis), (), 0, length) for axis, length in enumerate(result.shape)]
        where[longest] = (where[longest] + shift) % result.shape[longest]
        spots.append(tuple(where))
    return result.at[spots[0]].set(smallest).at[spots[1]].set(top_value)


def block_scale(own_key, extent, cuts, least, largest):
    def one(position, blocks):
        steps = jax.random.uniform(jax.random.fold_in(jax.random.fold_in(own_key, 6), position), (blocks,), jnp.float32, least / len(cuts), largest / len(cuts))
        return jnp.repeat(jnp.exp(steps), extent[position] // blocks).reshape((-1,) + (1,) * (len(extent) - position - 1))

    factor_of = one(*cuts[0])
    for cut in cuts[1:]:
        factor_of = factor_of * one(*cut)
    return factor_of


def assign_block(key, own, number, rows, count, top, limit, skew):
    ranking = jax.random.permutation(key, count)
    crowded, common = shares(count, rows * top, limit, skew, True), shares(count, rows * top, limit, skew, False)
    places = jnp.arange(count)

    def named(lengths, rotation):
        used = int((lengths > 0).sum())
        fixed = max(1, used // 4)
        moved = fixed + (places - fixed + rotation * (used - fixed)) % max(1, count - fixed)
        return jnp.zeros((count,), jnp.int32).at[ranking[jnp.where(places < fixed, places, moved)]].set(jnp.asarray(lengths, jnp.int32))

    lengths = jnp.where(number % 4 == 0, named(crowded, number // 4), named(common, number - number // 4 - 1))
    mixed = jax.random.permutation(jax.random.fold_in(own, 3), count)
    source_of, receiver = mixed[0:count // 2 * 2:2], mixed[1:count // 2 * 2:2]
    slack = jnp.minimum(lengths[source_of] - 1, limit - lengths[receiver]) // 2
    slack = jnp.where((source_of == ranking[0]) | (receiver == ranking[0]) | (lengths[receiver] == 0), 0, jnp.maximum(slack, 0))
    moved = jax.random.randint(jax.random.fold_in(own, 4), (count // 2,), 0, 1 << 20) % (slack + 1)
    lengths = lengths.at[source_of].add(-moved).at[receiver].add(moved)
    labels = jnp.searchsorted(jnp.cumsum(lengths), jnp.arange(rows * top), side="right").astype(jnp.int32)
    table = labels.reshape(top, rows).T
    table = table[jax.random.permutation(jax.random.fold_in(own, 1), rows)]
    rotation = jax.random.randint(jax.random.fold_in(own, 2), (rows, 1), 0, top)
    return jnp.take_along_axis(table, (jnp.arange(top)[None, :] + rotation) % top, axis=1)


def shares(number_of, total, most, skew, full):
    portions = [(1 << 20) // math.isqrt(standing ** skew) + 1 for standing in range(1, number_of + 1)]
    largest = most if full else min(most, max(-(-total // number_of), total * portions[0] // sum(portions)))
    least = 1 if total - largest >= number_of - 1 else 0
    holding, rest = [largest] + [least] * (number_of - 1), total - largest - least * (number_of - 1)
    while rest > 0:
        free = [i for i in range(1, number_of) if holding[i] < largest] or [i for i in range(1, number_of) if holding[i] < most]
        mass, left = sum([portions[i] for i in free]), rest
        for i in free:
            addition = min(most - holding[i], max(1, left * portions[i] // mass), rest)
            holding[i] = holding[i] + addition
            rest = rest - addition
    return np.array(holding)


def bell_draw(key, dims, spread, reach, cuts=(), kind=jnp.bfloat16):
    array = jax.random.normal(key, dims, jnp.float32) * spread
    if len(cuts) > 0:
        array = block_scale(key, dims, cuts, -0.22, 0.18) * array
    return jnp.clip(array, min=-reach, max=reach).astype(kind)


def setup_inputs(seed: int = 0) -> dict:
    splits = jax.random.split(jax.random.key(seed), 13)
    feats = bell_draw(splits[0], (TOKENS, 3, D), 1.0, 6.0, ((0, 2), (2, 64)))
    ids = touch_ends(jax.random.randint(splits[1], (TOKENS,), 0, VOCAB), jax.random.fold_in(splits[1], 1), 0, VOCAB - 1).astype(jnp.int32)
    loss_mask = touch_ends((jax.random.randint(splits[2], (TOKENS,), 0, 4) < 3).astype(jnp.int32), jax.random.fold_in(splits[2], 1), 0, 1)
    owner_keys = jax.random.split(jax.random.fold_in(splits[3], 1), (N_SEQ * NBLK) // NBLK)
    owner_turns = jax.random.permutation(jax.random.fold_in(splits[3], 3), (N_SEQ * NBLK) // NBLK)
    owner = jax.vmap(lambda own, number: assign_block(jax.random.fold_in(splits[3], 2), own, number, NBLK, N_SEQ, 1, MOST, 2))(owner_keys, owner_turns).reshape((N_SEQ * NBLK, 1))
    shifts = jax.random.randint(splits[4], (STEPS,), 0, BLK).astype(jnp.int32)
    target_gain = jnp.clip(1.0 + 0.1 * jax.random.normal(splits[5], (D,), jnp.float32), 0.5, 1.5).astype(jnp.bfloat16)
    target_head = draw_target_head(jax.random.fold_in(splits[12], 71), 0)
    fc_weight = bell_draw(splits[7], (3 * D, D), (3 * D) ** -0.5, 0.0390625, ((0, 2), (1, 64)))
    embed = bell_draw(splits[8], (VOCAB, D), 1.0, 6.0, ((0, 2), (1, 64)))
    draft_gain = jnp.clip(1.0 + 0.1 * jax.random.normal(splits[9], (D,), jnp.float32), 0.5, 1.5).astype(jnp.bfloat16)
    layer_weight = bell_draw(splits[10], (D, D), D ** -0.5, 0.0625, ((1, 64),))
    draft_head = draw_draft_head(jax.random.fold_in(splits[12], 71), 0)
    return {"feats": feats, "ids": ids, "loss_mask": loss_mask, "owner": owner, "shifts": shifts, "target_gain": target_gain, "target_head": target_head, "fc_weight": fc_weight, "embed": embed, "draft_gain": draft_gain, "layer_weight": layer_weight, "draft_head": draft_head}


def normalize(values):
    return values * lax.rsqrt(lax.optimization_barrier(jnp.mean(values * values, axis=-1, keepdims=True)) + 1e-05)

def entropy_part(target):
    positive = target > 0
    return jnp.where(positive, target * jnp.log(jnp.where(positive, target, 1.0)), 0.0)

def reference(feats, ids, loss_mask, owner, shifts, target_gain, target_head, fc_weight, embed, draft_gain, layer_weight, draft_head):
    high_rows = feats[:, 2, :].astype(jnp.float32)
    target_rows = (normalize(high_rows) * target_gain.astype(jnp.float32)).astype(jnp.bfloat16)
    target_logits = jnp.dot(target_rows, target_head, preferred_element_type=jnp.float32)
    peak_val = lax.optimization_barrier(jnp.max(target_logits, axis=1, keepdims=True))
    exp_terms = jnp.exp(target_logits - peak_val)
    target_probs = (exp_terms / lax.optimization_barrier(jnp.sum(exp_terms, axis=1, keepdims=True))).astype(jnp.bfloat16)
    united = jnp.dot(feats.reshape(TOKENS, 3 * D), fc_weight, preferred_element_type=jnp.float32).astype(jnp.bfloat16)
    positions = jnp.arange(TOKENS, dtype=jnp.int32)
    block_start = positions // BLK * BLK
    within = positions % BLK
    mask_float = loss_mask.astype(jnp.float32)
    weights = mask_float * (VOCAB / (STEPS * BLK))
    hidden_state = united.astype(jnp.float32)
    total_grad = jnp.zeros((D, VOCAB), jnp.float32)
    scores = []
    for turn_index in range(STEPS):
        source_pos = (block_start + (within + shifts[turn_index]) % BLK).astype(jnp.int32)
        embedded = jnp.take(embed, jnp.take(ids, source_pos, axis=0), axis=0).astype(jnp.float32)
        mixed = (hidden_state + embedded).astype(jnp.bfloat16)
        normed = (normalize(mixed.astype(jnp.float32)) * draft_gain.astype(jnp.float32)).astype(jnp.bfloat16)
        if turn_index + 1 < STEPS:
            hidden_state = hidden_state + jax.nn.silu(jnp.dot(normed, layer_weight, preferred_element_type=jnp.float32))
        logits = jnp.dot(normed, draft_head, preferred_element_type=jnp.float32)
        target = jnp.take(target_probs, source_pos, axis=0).astype(jnp.float32)
        peak_row = lax.optimization_barrier(jnp.max(logits, axis=1, keepdims=True))
        draft_exp = jnp.exp(logits - peak_row)
        totals = lax.optimization_barrier(jnp.sum(draft_exp, axis=1, keepdims=True))
        log_soft = logits - peak_row - jnp.log(totals)
        prob_mass = lax.optimization_barrier(jnp.sum(target, axis=1, keepdims=True))
        kl_terms = lax.optimization_barrier(jnp.sum(entropy_part(target) - target * log_soft, axis=1))
        soft_probs = draft_exp / totals
        grad_logits = (weights[:, None] * (soft_probs * prob_mass - target)).astype(jnp.bfloat16)
        total_grad = total_grad + jnp.dot(normed.T, grad_logits, preferred_element_type=jnp.float32)
        scores.append(kl_terms * mask_float)
    kl_all = jnp.stack(scores)
    owners = owner[:, 0].reshape(N_SEQ, NBLK)
    seq_ids = jnp.arange(N_SEQ, dtype=jnp.int32)
    owner_hits = (owners[:, :, None] == seq_ids[None, None, :]).astype(jnp.int32)
    owner_rank = lax.optimization_barrier(jnp.sum((jnp.cumsum(owner_hits, axis=1) - 1) * owner_hits, axis=2))
    dest_block = owners * (N_SEQ * MOST) + seq_ids[:, None] * MOST + owner_rank
    dest_index = (dest_block.reshape(-1)[:, None] * BLK + jnp.arange(BLK, dtype=jnp.int32)[None, :]).reshape(-1)
    slot_kl = jnp.zeros((STEPS, N_SEQ * N_SEQ * MOST * BLK), jnp.float32).at[:, dest_index].set(kl_all)
    return (total_grad.astype(jnp.bfloat16), slot_kl)
```

```python
import functools

import jax
import jax.numpy as jnp
import numpy as np
from jax import lax
from jax.experimental import pallas as pl
from jax.experimental.pallas import tpu as pltpu
from jax.sharding import Mesh
from jax.sharding import PartitionSpec as P

BLK = 16
STEPS = 3
MOST = 6
LANE = 128
HALF = 64
TOK = 128
EPS = 1e-05

VMEM = pl.BlockSpec(memory_space=pltpu.VMEM)
SMEM = pl.BlockSpec(memory_space=pltpu.SMEM)
F32 = jnp.float32
BF16 = jnp.bfloat16


def call(kernel, outs, ins, *, flops=0, nbytes=0, scratch=()):
    return pl.pallas_call(
        kernel,
        out_shape=outs,
        in_specs=list(ins),
        out_specs=jax.tree.map(lambda _: VMEM, outs),
        scratch_shapes=list(scratch),
        compiler_params=pltpu.CompilerParams(vmem_limit_bytes=48 * 1024 * 1024),
        cost_estimate=pl.CostEstimate(flops=flops, bytes_accessed=nbytes, transcendentals=0),
    )


def sds(shape, dtype):
    return jax.ShapeDtypeStruct(shape, dtype)


def dot(a, b):
    return jnp.dot(a, b, preferred_element_type=F32)


def spread(values, axis):
    count = lax.axis_size(axis)
    return lax.all_to_all(
        jnp.broadcast_to(values[None], (count,) + values.shape), axis, 0, 0, tiled=True
    )


def swap(values, axis):
    count = lax.axis_size(axis)
    return lax.ppermute(values, axis, [(i, (i + count // 2) % count) for i in range(count)])


def shift_matrix(shift, rows):
    src = lax.broadcasted_iota(jnp.int32, (rows, rows), 0)
    tok = lax.broadcasted_iota(jnp.int32, (rows, rows), 1)
    want = (tok & ~(BLK - 1)) + ((tok & (BLK - 1)) + shift & (BLK - 1))
    return jnp.where(src == want, 1.0, 0.0).astype(BF16)


def shift_rows(shift, rows):
    tok = lax.broadcasted_iota(jnp.int32, (rows, rows), 0)
    src = lax.broadcasted_iota(jnp.int32, (rows, rows), 1)
    want = (tok & ~(BLK - 1)) + ((tok & (BLK - 1)) + shift & (BLK - 1))
    return jnp.where(src == want, 1.0, 0.0).astype(BF16)


def split3(x):
    hi = x.astype(BF16)
    rest = x - hi.astype(F32)
    mid = rest.astype(BF16)
    low = (rest - mid.astype(F32)).astype(BF16)
    return hi, mid, low


def unite_kernel(pos_ref, x_ref, fc_ref, own_ref, other_ref, acc_ref):
    g = pos_ref[0]
    whole = pl.multiple_of(g * 4096, 4096)
    middle = pl.multiple_of((1 - g) * 8192, 4096)
    acc = jnp.zeros((TOK, LANE), F32)
    for i in range(4):
        lhs = jnp.concatenate([x_ref[i * 16 + j, 0:TOK, :] for j in range(16)], axis=1)
        acc += dot(lhs, fc_ref[pl.ds(whole + i * 2048, 2048), :])
    acc_ref[...] = acc
    for h in range(2):
        part = jnp.zeros((HALF, LANE), F32)
        for i in range(2):
            lhs = jnp.concatenate(
                [x_ref[h * 32 + i * 16 + j, TOK : TOK + HALF, :] for j in range(16)], axis=1
            )
            part += dot(lhs, fc_ref[pl.ds(middle + i * 2048, 2048), :])
        acc_ref[h * HALF : (h + 1) * HALF, :] += part
    own_ref[...] = acc_ref[pl.ds(pl.multiple_of(g * HALF, HALF), HALF), :]
    other_ref[...] = acc_ref[pl.ds(pl.multiple_of((1 - g) * HALF, HALF), HALF), :]


def first_kernel(shifts_ref, own_ref, got_ref, e_own_ref, e_got_ref, state_ref, e_ref, mix_ref):
    state = (own_ref[...] + got_ref[...]).astype(BF16).astype(F32)
    state_ref[...] = state
    rows = (e_own_ref[...].astype(F32) + e_got_ref[...].astype(F32)).astype(BF16)
    e_ref[...] = rows
    mixed = (state + dot(shift_rows(shifts_ref[0], HALF), rows)).astype(BF16)
    for i in range(8):
        mix_ref[i] = mixed


def normalize_into(x_of, gain_ref, count, rows, out_of):
    total = jnp.zeros((rows, LANE), F32)
    for p in range(count):
        v = x_of(p).astype(F32)
        total += v * v
    scale = lax.rsqrt(jnp.sum(total, axis=1, keepdims=True) / (count * LANE) + EPS)
    for i in range(count // 16):
        gain = gain_ref[i].astype(F32)
        for j in range(16):
            p = i * 16 + j
            out_of(p, (x_of(p).astype(F32) * scale * gain[j : j + 1, :]).astype(BF16))


def row_dot(n_of, w_ref, rows):
    acc = jnp.zeros((rows, LANE), F32)
    for i in range(4):
        lhs = jnp.concatenate([n_of(i * 16 + j) for j in range(16)], axis=1)
        acc += dot(lhs, w_ref[i * 2048 : (i + 1) * 2048, :])
    return acc


def layer_kernel(step, shifts_ref, x_ref, gain_ref, w_ref, state_ref, e_ref, n_ref, next_ref, mix_ref):
    def put(p, value):
        n_ref[p] = value

    normalize_into(lambda p: x_ref[p], gain_ref, 64, HALF, put)
    acc = row_dot(lambda p: n_ref[p], w_ref, HALF)
    state = state_ref[...] + acc * jax.nn.sigmoid(acc)
    next_ref[...] = state
    mixed = (state + dot(shift_rows(shifts_ref[step + 1], HALF), e_ref[...])).astype(BF16)
    for i in range(mix_ref.shape[0]):
        mix_ref[i] = mixed


def target_kernel(x_ref, gain_ref, w_ref, logits_ref, stat_ref, n_ref):
    def put(p, value):
        n_ref[p] = value

    normalize_into(lambda p: x_ref[p], gain_ref, 64, TOK, put)
    logits = row_dot(lambda p: n_ref[p], w_ref, TOK).T
    logits_ref[...] = logits
    peak = jnp.max(logits, axis=0, keepdims=True)
    total = jnp.sum(jnp.exp(logits - peak), axis=0, keepdims=True)
    parts = list(split3(peak)) + list(split3(total))
    rows = jnp.concatenate(
        [v.astype(F32) for v in parts] + [jnp.zeros((10, LANE), F32)], axis=0
    )
    stat_ref[...] = rows.astype(BF16)


def logits_kernel(
    pos_ref,
    shifts_ref,
    x_ref,
    tstat_ref,
    gain_ref,
    w_ref,
    a0_ref,
    b0_ref,
    a1_ref,
    b1_ref,
    t_ref,
    n_ref,
    l_ref,
    p_ref,
    stat_ref,
    rows_ref,
):
    g = pos_ref[0]
    for h in range(2):

        def put(p, value, h=h):
            n_ref[p, h * HALF : (h + 1) * HALF, :] = value

        normalize_into(lambda p, h=h: x_ref[h, p], gain_ref, 64, HALF, put)
    peaks = tstat_ref[:, 0].astype(F32) + tstat_ref[:, 1].astype(F32) + tstat_ref[:, 2].astype(F32)
    totals = tstat_ref[:, 3].astype(F32) + tstat_ref[:, 4].astype(F32) + tstat_ref[:, 5].astype(F32)
    peak = jnp.max(peaks, axis=0, keepdims=True)
    total = jnp.sum(totals * jnp.exp(peaks - peak), axis=0, keepdims=True)
    probs = (jnp.exp(t_ref[...] - peak) / total).astype(BF16)
    own = pl.ds(pl.multiple_of(g * HALF, HALF), HALF)
    other = pl.ds(pl.multiple_of((1 - g) * HALF, HALF), HALF)
    stats = []
    for k in range(STEPS):
        if k == 2:
            logits = row_dot(lambda p: n_ref[p], w_ref, TOK)
        else:
            mine, theirs = ((a0_ref, b0_ref), (a1_ref, b1_ref))[k]
            rows_ref[own, :] = row_dot(lambda p: mine[p], w_ref, HALF)
            rows_ref[other, :] = row_dot(lambda p: theirs[p], w_ref, HALF)
            logits = rows_ref[...]
        logits = logits.T
        l_ref[k] = logits
        target = dot(probs, shift_matrix(shifts_ref[k], TOK))
        p_ref[k] = target.astype(BF16)
        peak = jnp.max(logits, axis=0, keepdims=True)
        total = jnp.sum(jnp.exp(logits - peak), axis=0, keepdims=True)
        positive = target > 0
        entropy = jnp.where(positive, target * jnp.log(jnp.where(positive, target, 1.0)), 0.0)
        cross = jnp.sum(entropy - target * logits, axis=0, keepdims=True)
        mass = jnp.sum(target, axis=0, keepdims=True)
        stats += [peak, total, cross, mass]
    rows = jnp.concatenate(stats + [jnp.zeros((4, LANE), F32)], axis=0)
    for i in range(8):
        stat_ref[i] = rows


def combine(blocks):
    rows = []
    for k in range(STEPS):
        peaks = blocks[:, 4 * k, :]
        peak = jnp.max(peaks, axis=0, keepdims=True)
        total = jnp.sum(blocks[:, 4 * k + 1, :] * jnp.exp(peaks - peak), axis=0, keepdims=True)
        cross = jnp.sum(blocks[:, 4 * k + 2, :], axis=0, keepdims=True)
        mass = jnp.sum(blocks[:, 4 * k + 3, :], axis=0, keepdims=True)
        rows.append((peak, total, cross, mass))
    return rows


def middle_kernel(in_ref, out_ref):
    rows = []
    for item in combine(in_ref[...]):
        rows += list(item)
    rows = jnp.concatenate(rows + [jnp.zeros((4, LANE), F32)], axis=0)
    for i in range(16):
        out_ref[i] = rows


def grad_kernel(vocab_total, pos_ref, in_ref, mask_ref, l_ref, p_ref, grad_ref, kl_ref):
    g = pos_ref[0]
    mask = mask_ref[...]
    weight = mask * (vocab_total / (STEPS * BLK))
    scores = []
    for k, (peak, total, cross, mass) in enumerate(combine(in_ref[...])):
        soft = jnp.exp(l_ref[k] - peak) / total
        grad = weight * (soft * mass - p_ref[k].astype(F32))
        if k < 2:
            grad = pltpu.roll(grad, g * HALF, 1)
        grad_ref[k] = grad.astype(BF16)
        scores.append((cross + (peak + jnp.log(total)) * mass) * mask)
    kl_ref[...] = jnp.concatenate(scores + [jnp.zeros((5, LANE), F32)], axis=0)


def head_kernel(
    pos_ref, g_ref, h_ref, a0_ref, b0_ref, a1_ref, b1_ref, n2_ref, c0_ref, d0_ref, c1_ref, d1_ref, m2_ref, out_ref
):
    first = pos_ref[1] * 32
    lhs = jnp.concatenate(
        [g_ref[0], g_ref[1], g_ref[2], h_ref[0], h_ref[1], h_ref[2]], axis=1
    )

    def body(q, carry):
        p = first + q
        rhs = jnp.concatenate(
            [
                a0_ref[p],
                b0_ref[p],
                a1_ref[p],
                b1_ref[p],
                n2_ref[p],
                c0_ref[q],
                d0_ref[q],
                c1_ref[q],
                d1_ref[q],
                m2_ref[q],
            ],
            axis=0,
        )
        out_ref[q] = dot(lhs, rhs).T.astype(BF16)
        return carry

    lax.fori_loop(0, 32, body, 0, unroll=4)


def on_device(
    feats,
    ids,
    loss_mask,
    owner,
    shifts,
    target_gain,
    target_head,
    fc_weight,
    embed,
    draft_gain,
    layer_weight,
    draft_head,
):
    g = lax.axis_index("xh")
    c = lax.axis_index("c")
    y_half = lax.axis_index("y") // 2
    pos = jnp.stack([g, c]).astype(jnp.int32)
    vocab_total = LANE * 128
    target_gain = target_gain.reshape(4, 16, LANE)
    draft_gain = draft_gain.reshape(4, 16, LANE)

    mid = feats[:, 1, :].reshape(2, HALF, LANE)
    mid_own = lax.dynamic_index_in_dim(mid, y_half, 0, keepdims=False)
    mid_send = lax.dynamic_index_in_dim(mid, 1 - y_half, 0, keepdims=False)
    mid_got = swap(mid_send, "y")

    seq_ids = lax.dynamic_slice_in_dim(ids, c * TOK, TOK, 0)
    local_ids = seq_ids - g * embed.shape[0]
    inside = (local_ids >= 0) & (local_ids < embed.shape[0])
    picked = jnp.take(embed, jnp.clip(local_ids, 0, embed.shape[0] - 1), axis=0)
    picked = jnp.where(inside[:, None], picked, jnp.zeros((), BF16)).reshape(2, HALF, LANE)
    e_own = lax.dynamic_index_in_dim(picked, g, 0, keepdims=False)
    e_got = swap(lax.dynamic_index_in_dim(picked, 1 - g, 0, keepdims=False), "xh")

    level = jnp.where(g == 0, feats[:, 0, :], feats[:, 2, :])
    piece = jnp.where(y_half == g, mid_own, mid_got)
    load = jnp.concatenate([level, piece], axis=0)
    wide = spread(load, "z").reshape(8 * 192, LANE)
    wide = spread(wide, ("y", "xl")).reshape(64, 192, LANE)

    own_part, other_part = call(
        unite_kernel,
        (sds((HALF, LANE), F32), sds((HALF, LANE), F32)),
        (SMEM, VMEM, VMEM),
        flops=2 * 128 * 12288 * 128,
        nbytes=6 << 20,
        scratch=[pltpu.VMEM((TOK, LANE), F32)],
    )(pos, wide, fc_weight)
    part_got = swap(other_part, "xh")

    high_own = wide[:, :TOK, :]
    high_got = lax.ppermute(high_own, "xh", [(1, 0)])

    state, e_rows, mix = call(
        first_kernel,
        (sds((HALF, LANE), F32), sds((HALF, LANE), BF16), sds((8, HALF, LANE), BF16)),
        (SMEM, VMEM, VMEM, VMEM, VMEM),
    )(shifts, own_part, part_got, e_own, e_got)

    mine, theirs = [], []
    for step in range(2):
        part = lax.all_to_all(mix, "z", 0, 0, tiled=True).reshape(8 * HALF, LANE)
        rows = spread(part, ("y", "xl")).reshape(64, HALF, LANE)
        normed, state, mix = call(
            functools.partial(layer_kernel, step),
            (
                sds((64, HALF, LANE), BF16),
                sds((HALF, LANE), F32),
                sds((8 if step == 0 else 1, HALF, LANE), BF16),
            ),
            (SMEM, VMEM, VMEM, VMEM, VMEM, VMEM),
            flops=2 * 64 * 8192 * 128,
            nbytes=4 << 20,
        )(shifts, rows, draft_gain, layer_weight, state, e_rows)
        mine.append(normed)
        theirs.append(swap(normed, "xh"))

    high = jnp.where(g == 0, high_got, high_own)
    t_logits, t_stat = call(
        target_kernel,
        (sds((LANE, TOK), F32), sds((16, LANE), BF16)),
        (VMEM, VMEM, VMEM),
        flops=2 * 128 * 8192 * 128,
        nbytes=4 << 20,
        scratch=[pltpu.VMEM((64, TOK, LANE), BF16)],
    )(high, target_gain, target_head)

    load = jnp.concatenate([mix[0], t_stat], axis=0)
    part = spread(load, "z").reshape(8 * 80, LANE)
    last = spread(part, ("xh", "y", "xl")).reshape(2, 64, 80, LANE)
    last_rows = last[:, :, :HALF]
    last_stat = last[:, :, HALF:].reshape(128, 16, LANE)

    n_last, logits, probs, stat = call(
        logits_kernel,
        (
            sds((64, TOK, LANE), BF16),
            sds((STEPS, LANE, TOK), F32),
            sds((STEPS, LANE, TOK), BF16),
            sds((8, 16, LANE), F32),
        ),
        (SMEM, SMEM) + (VMEM,) * 9,
        flops=6 * 128 * 8192 * 128,
        nbytes=10 << 20,
        scratch=[pltpu.VMEM((TOK, LANE), F32)],
    )(
        pos,
        shifts,
        last_rows,
        last_stat,
        draft_gain,
        draft_head,
        mine[0],
        theirs[0],
        mine[1],
        theirs[1],
        t_logits,
    )

    def from_other(values):
        rows = values.shape[1]
        half = lax.dynamic_slice(values, ((1 - c) * 32, 0, 0), (32, rows, LANE))
        return swap(half, "c")

    across = [from_other(v) for v in (mine[0], theirs[0], mine[1], theirs[1], n_last)]

    stat = lax.all_to_all(stat, "z", 0, 0, tiled=True)
    stat = call(middle_kernel, sds((16, 16, LANE), F32), (VMEM,))(stat)
    stat = lax.all_to_all(stat, ("xh", "y", "xl"), 0, 0, tiled=True)

    mask = lax.dynamic_slice_in_dim(loss_mask, c * TOK, TOK, 0).astype(F32)[None, :]
    grads, kl = call(
        functools.partial(grad_kernel, vocab_total),
        (sds((STEPS, LANE, TOK), BF16), sds((8, LANE), F32)),
        (SMEM,) + (VMEM,) * 4,
    )(pos, stat, mask, logits, probs)
    grads_got, kl_got = swap(grads, "c"), swap(kl, "c")

    head_grad = call(
        head_kernel,
        sds((32, LANE, LANE), BF16),
        (SMEM,) + (VMEM,) * 12,
        flops=2 * 768 * 4096 * 128,
        nbytes=8 << 20,
    )(
        pos,
        grads,
        grads_got,
        mine[0],
        theirs[0],
        mine[1],
        theirs[1],
        n_last,
        *across,
    ).reshape(4096, LANE)

    blocks = TOK // BLK
    kl_own, kl_other = kl[:STEPS], kl_got[:STEPS]
    kl_all = jnp.where(c == 0, jnp.stack([kl_own, kl_other], 1), jnp.stack([kl_other, kl_own], 1))
    kl_all = kl_all.reshape(STEPS, 2, 1, blocks, BLK)
    hits = (owner[:, 0].reshape(2, blocks) == c).astype(jnp.int32)
    rank = jnp.cumsum(hits, axis=1) - 1
    pick = (hits[:, None, :] > 0) & (
        rank[:, None, :] == jnp.arange(MOST, dtype=jnp.int32)[None, :, None]
    )
    slot_kl = jnp.sum(jnp.where(pick[None, :, :, :, None], kl_all, 0.0), axis=3)
    return head_grad, slot_kl.reshape(STEPS, 2 * MOST * BLK)


def solution(mesh):
    fine = Mesh(np.asarray(mesh.devices).reshape(2, 4, 2, 8, 2), ("xh", "y", "xl", "z", "c"))
    tp = ("y", "xl", "z")
    every = ("xh",) + tp
    return jax.shard_map(
        on_device,
        mesh=fine,
        in_specs=(
            P("c", None, tp),
            P(),
            P(),
            P(),
            P(),
            P(),
            P(None, every),
            P("xh", tp),
            P("xh", tp),
            P(),
            P(None, tp),
            P(None, every),
        ),
        out_specs=(P("c", every), P(None, "c")),
        check_vma=False,
    )
```

```python
import functools

import jax
import jax.numpy as jnp
import numpy as np
from jax import lax
from jax.experimental import pallas as pl
from jax.experimental.pallas import tpu as pltpu
from jax.sharding import Mesh
from jax.sharding import PartitionSpec as P

BLK = 16
STEPS = 3
MOST = 6
LANE = 128
HALF = 64
TOK = 128
EPS = 1e-05

VMEM = pl.BlockSpec(memory_space=pltpu.VMEM)
SMEM = pl.BlockSpec(memory_space=pltpu.SMEM)
ANY = pl.BlockSpec(memory_space=pl.ANY)
F32 = jnp.float32
BF16 = jnp.bfloat16


def call(kernel, outs, ins, *, flops=0, nbytes=0, scratch=(), sems=0, far=(), big=True):
    return pl.pallas_call(
        kernel,
        out_shape=tuple(outs),
        in_specs=list(ins),
        out_specs=tuple(ANY if i in far else VMEM for i in range(len(outs))),
        scratch_shapes=list(scratch) + ([pltpu.SemaphoreType.DMA((sems,))] if sems else []),
        compiler_params=pltpu.CompilerParams(vmem_limit_bytes=(60 if big else 4) * 1024 * 1024),
        cost_estimate=pl.CostEstimate(flops=flops, bytes_accessed=nbytes, transcendentals=0),
    )


def sds(shape, dtype):
    return jax.ShapeDtypeStruct(shape, dtype)


def begin(source, target, sem):
    copy = pltpu.make_async_copy(source, target, sem)
    copy.start()
    return copy


def dot(a, b):
    return jnp.dot(a, b, preferred_element_type=F32)


def spread(values, axis):
    count = lax.axis_size(axis)
    return lax.all_to_all(
        jnp.broadcast_to(values[None], (count,) + values.shape), axis, 0, 0, tiled=True
    )


def across_grp(values, pairs=((0, 3), (1, 2), (2, 1), (3, 0))):
    return lax.ppermute(values, ("xh", "xl"), list(pairs))


def swap(values, axis):
    count = lax.axis_size(axis)
    return lax.ppermute(values, axis, [(i, (i + count // 2) % count) for i in range(count)])


def shift_lanes(values, shift):
    place = lax.broadcasted_iota(jnp.int32, values.shape, 1) & (BLK - 1)
    ahead = pltpu.roll(values, (TOK - shift) & (TOK - 1), 1)
    return jnp.where(place + shift < BLK, ahead, pltpu.roll(values, BLK - shift, 1))


def shift_rows(shift, rows):
    tok = lax.broadcasted_iota(jnp.int32, (rows, rows), 0)
    src = lax.broadcasted_iota(jnp.int32, (rows, rows), 1)
    want = (tok & ~(BLK - 1)) + ((tok & (BLK - 1)) + shift & (BLK - 1))
    return jnp.where(src == want, 1.0, 0.0).astype(BF16)


def unite_kernel(pos_ref, a_ref, *rest):
    ring, (fc_ref, own_ref, other_ref, x_ref, w_ref, m_ref, v_ref, acc_ref, sem) = rest[:9], rest[9:]
    g, z = pos_ref[0], pos_ref[2]
    whole = pl.multiple_of(g * 4096, 4096)
    middle = pl.multiple_of((1 - g) * 8192, 4096)
    first = []
    for i in range(4):
        rows = pl.ds(whole + i * 2048, 2048)
        first.append(begin(a_ref.at[pl.ds(i * 16, 16)], x_ref.at[pl.ds(i * 16, 16)], sem.at[2 * i]))
        first.append(begin(fc_ref.at[rows], w_ref.at[pl.ds(i * 2048, 2048)], sem.at[2 * i + 1]))
    second = [begin(fc_ref.at[pl.ds(middle, 4096)], v_ref, sem.at[8])]
    for n, (ref, away) in enumerate(zip(ring[:7], (0, -1, 1, -2, 2, -3, 3))):
        second.append(begin(ref, m_ref.at[(z + away + 8) & 7], sem.at[9 + n]))
    second.append(begin(ring[7], m_ref.at[(z + 4) & 7, pl.ds(0, 1)], sem.at[16]))
    second.append(begin(ring[8], m_ref.at[(z + 4) & 7, pl.ds(1, 1)], sem.at[17]))
    acc = jnp.zeros((TOK, LANE), F32)
    for i in range(4):
        first[2 * i].wait()
        first[2 * i + 1].wait()
        lhs = jnp.concatenate([x_ref[i * 16 + j] for j in range(16)], axis=1)
        acc += dot(lhs, w_ref[i * 2048 : (i + 1) * 2048, :])
    for copy in second:
        copy.wait()
    for yl in range(2):
        for xl in range(2):
            lhs = jnp.concatenate([m_ref[j, xl, yl] for j in range(8)], axis=1)
            at = (yl * 2 + xl) * 1024
            acc += dot(lhs, v_ref[at : at + 1024, :])
    acc_ref[...] = acc
    own_ref[...] = acc_ref[pl.ds(pl.multiple_of(g * HALF, HALF), HALF), :]
    other_ref[...] = acc_ref[pl.ds(pl.multiple_of((1 - g) * HALF, HALF), HALF), :]


def first_kernel(shifts_ref, own_ref, got_ref, e_own_ref, e_got_ref, state_ref, e_ref, mix_ref):
    state = (own_ref[...] + got_ref[...]).astype(BF16).astype(F32)
    state_ref[...] = state
    rows = (e_own_ref[...].astype(F32) + e_got_ref[...].astype(F32)).astype(BF16)
    e_ref[...] = rows
    mixed = (state + dot(shift_rows(shifts_ref[0], HALF), rows)).astype(BF16)
    for i in range(64):
        mix_ref[i] = mixed


def normalize_into(x_of, gain_ref, count, rows, out_of, ready=None):
    total = jnp.zeros((rows, LANE), F32)
    for p in range(count):
        if ready is not None and p % 16 == 0:
            for copy in ready[p // 16]:
                copy.wait()
        v = x_of(p).astype(F32)
        total += v * v
    scale = lax.rsqrt(jnp.sum(total, axis=1, keepdims=True) / (count * LANE) + EPS)
    for i in range(count // 16):
        gain = gain_ref[i].astype(F32)
        for j in range(16):
            p = i * 16 + j
            out_of(p, (x_of(p).astype(F32) * scale * gain[j : j + 1, :]).astype(BF16))


def row_dot(n_of, w_ref, rows):
    acc = jnp.zeros((rows, LANE), F32)
    for i in range(4):
        lhs = jnp.concatenate([n_of(i * 16 + j) for j in range(16)], axis=1)
        acc += dot(lhs, w_ref[i * 2048 : (i + 1) * 2048, :])
    return acc


def layer_kernel(
    step,
    pos_ref,
    shifts_ref,
    far_x_ref,
    gain_ref,
    far_w_ref,
    state_ref,
    e_ref,
    low_ref,
    high_ref,
    half_ref,
    next_ref,
    mix_ref,
    x_ref,
    w_ref,
    n_ref,
    sem,
):
    ready = []
    for i in range(4):
        part = pl.ds(i * 16, 16)
        ready.append([begin(far_x_ref.at[part], x_ref.at[part], sem.at[i])])
    weights = begin(far_w_ref, w_ref, sem.at[4])

    def put(p, value):
        n_ref[p] = value

    normalize_into(lambda p: x_ref[p], gain_ref, 64, HALF, put, ready)
    low = begin(n_ref.at[pl.ds(0, 32)], low_ref, sem.at[5])
    high = begin(n_ref.at[pl.ds(32, 32)], high_ref, sem.at[7])
    half = begin(n_ref.at[pl.ds((1 - pos_ref[1]) * 32, 32)], half_ref, sem.at[6])
    weights.wait()
    acc = row_dot(lambda p: n_ref[p], w_ref, HALF)
    state = state_ref[...] + acc * jax.nn.sigmoid(acc)
    next_ref[...] = state
    mixed = (state + dot(shift_rows(shifts_ref[step + 1], HALF), e_ref[...])).astype(BF16)
    if step == 0:
        for i in range(64):
            mix_ref[i] = mixed
    else:
        for i in range(8):
            mix_ref[i] = mixed
    low.wait()
    high.wait()
    half.wait()


def target_kernel(
    pos_ref, own_ref, got_ref, gain_ref, far_w_ref, logits_ref, x_ref, w_ref, n_ref, sem
):
    weights = begin(far_w_ref, w_ref, sem.at[4])
    here = pos_ref[0]
    for source, which in ((got_ref, 0), (own_ref, 1)):

        @pl.when(here == which)
        def _(source=source):
            for i in range(4):
                part = pl.ds(i * 16, 16)
                begin(source.at[part], x_ref.at[part], sem.at[i])

    ready = []
    for i in range(4):
        part = pl.ds(i * 16, 16)
        ready.append([pltpu.make_async_copy(own_ref.at[part], x_ref.at[part], sem.at[i])])

    def put(p, value):
        n_ref[p] = value

    normalize_into(lambda p: x_ref[p], gain_ref, 64, TOK, put, ready)
    weights.wait()
    logits = row_dot(lambda p: n_ref[p], w_ref, TOK).T
    logits_ref[...] = logits


def early_kernel(
    pos_ref, far_w_ref, a_low_ref, a_high_ref, b_low_ref, b_high_ref, l_ref, w_ref, a_ref, b_ref, rows_ref, sem
):
    low, high = pl.ds(0, 32), pl.ds(32, 32)
    copies = [
        begin(far_w_ref, w_ref, sem.at[0]),
        begin(a_low_ref, a_ref.at[low], sem.at[1]),
        begin(a_high_ref, a_ref.at[high], sem.at[2]),
        begin(b_low_ref, b_ref.at[low], sem.at[3]),
        begin(b_high_ref, b_ref.at[high], sem.at[4]),
    ]
    g = pos_ref[0]
    acc = jnp.zeros((TOK, LANE), F32)
    for i in range(4):
        for n in ((0, 1, 3), (), (2, 4), ())[i]:
            copies[n].wait()
        group = range(i * 16, i * 16 + 16)
        lhs = jnp.concatenate(
            [jnp.concatenate([ref[p] for p in group], axis=1) for ref in (a_ref, b_ref)], axis=0
        )
        acc += dot(lhs, w_ref[i * 2048 : (i + 1) * 2048, :])
    rows_ref[pl.ds(pl.multiple_of(g * HALF, HALF), HALF), :] = acc[:HALF]
    rows_ref[pl.ds(pl.multiple_of((1 - g) * HALF, HALF), HALF), :] = acc[HALF:]
    l_ref[...] = rows_ref[...].T


def logits_kernel(
    pos_ref,
    shifts_ref,
    far_x_ref,
    gain_ref,
    far_w_ref,
    l0_ref,
    l1_ref,
    t_ref,
    far_n_ref,
    half_ref,
    l_ref,
    tk_ref,
    stat_ref,
    x_ref,
    w_ref,
    n_ref,
    sem,
):
    ready = []
    for i in range(4):
        part = pl.ds(i * 16, 16)
        pair = []
        for h in range(2):
            rows = pl.ds(h * HALF, HALF)
            pair.append(begin(far_x_ref.at[h, part], x_ref.at[part, rows], sem.at[7 + 2 * i + h]))
        ready.append(pair)
    weights = begin(far_w_ref, w_ref, sem.at[4])

    def put(p, value):
        n_ref[p] = value

    normalize_into(lambda p: x_ref[p], gain_ref, 64, TOK, put, ready)
    out = begin(n_ref, far_n_ref, sem.at[5])
    half = begin(n_ref.at[pl.ds((1 - pos_ref[1]) * 32, 32)], half_ref, sem.at[6])
    weights.wait()
    l_ref[...] = row_dot(lambda p: n_ref[p], w_ref, TOK).T
    stats = []
    for k, ref in enumerate((l0_ref, l1_ref, l_ref)):
        logits, wanted = ref[...], shift_lanes(t_ref[...], shifts_ref[k])
        tk_ref[k] = wanted
        peak = jnp.max(logits, axis=0, keepdims=True)
        top = jnp.max(wanted, axis=0, keepdims=True)
        logits, wanted = logits - peak, wanted - top
        target = jnp.exp(wanted)
        total = jnp.sum(jnp.exp(logits), axis=0, keepdims=True)
        mass = jnp.sum(target, axis=0, keepdims=True)
        cross = jnp.sum(target * (wanted - logits), axis=0, keepdims=True)
        stats += [peak, total, top, mass, cross]
    rows = jnp.concatenate(stats + [jnp.zeros((1, LANE), F32)], axis=0)
    for i in range(8):
        stat_ref[i] = rows
    out.wait()
    half.wait()


def combine(blocks):
    rows = []
    for k in range(STEPS):
        peaks, totals, tops, masses, crosses = [blocks[:, 5 * k + i, :] for i in range(5)]
        peak = jnp.max(peaks, axis=0, keepdims=True)
        top = jnp.max(tops, axis=0, keepdims=True)
        total = jnp.sum(totals * jnp.exp(peaks - peak), axis=0, keepdims=True)
        share = jnp.exp(tops - top)
        mass = jnp.sum(masses * share, axis=0, keepdims=True)
        moved = crosses + masses * ((tops - top) - (peaks - peak))
        cross = jnp.sum(moved * share, axis=0, keepdims=True)
        rows.append((peak, total, top, mass, cross))
    return rows


def middle_kernel(in_ref, out_ref):
    rows = []
    for item in combine(in_ref[...]):
        rows += list(item)
    rows = jnp.concatenate(rows + [jnp.zeros((1, LANE), F32)], axis=0)
    for i in range(16):
        out_ref[i] = rows


def grad_kernel(vocab_total, pos_ref, in_ref, mask_ref, l0_ref, l1_ref, l2_ref, tk_ref, grad_ref, kl_ref):
    g = pos_ref[0]
    mask = mask_ref[...]
    weight = mask * (vocab_total / (STEPS * BLK))
    scores = []
    for k, (peak, total, top, mass, cross) in enumerate(combine(in_ref[...])):
        soft = jnp.exp((l0_ref, l1_ref, l2_ref)[k][...] - peak) / total
        target = (jnp.exp(tk_ref[k] - top) / mass).astype(BF16).astype(F32)
        grad = weight * (soft - target)
        if k < 2:
            grad = pltpu.roll(grad, g * HALF, 1)
        grad_ref[k] = grad.astype(BF16)
        scores.append((cross / mass - jnp.log(mass) + jnp.log(total)) * mask)
    kl_ref[...] = jnp.concatenate(scores + [jnp.zeros((5, LANE), F32)], axis=0)


def head_kernel(pos_ref, g_ref, h_ref, *rest):
    far, (out_ref, x_ref, o_ref, sem) = rest[:16], rest[16:]
    core = pos_ref[1]
    groups = (far[0:2], far[2:4], far[4:6], far[6:8], far[8:9], far[9:10], far[10:12], far[12:13], far[13:15], far[15:16])

    def copies_of(q, which):
        at, copies = 0, []
        for n, refs in enumerate(groups):
            ref = refs[which] if len(refs) == 2 else refs[0]
            count = ref.shape[1]
            start = q * 8 + (which * 32 if ref.shape[0] == 64 else 0)
            target = x_ref.at[pl.ds(q * 8, 8), pl.ds(at, count)]
            copies.append(pltpu.make_async_copy(ref.at[pl.ds(start, 8)], target, sem.at[q, n]))
            at += count
        return copies

    for which in range(2):

        @pl.when(core == which)
        def _(which=which):
            for q in range(4):
                for copy in copies_of(q, which):
                    copy.start()

    copies = [copies_of(q, 0) for q in range(4)]
    lhs = jnp.concatenate(
        [g_ref[0], g_ref[1], g_ref[2], h_ref[0], h_ref[1], h_ref[2]], axis=1
    )
    outs = []
    for q in range(4):
        for copy in copies[q]:
            copy.wait()
        rhs = jnp.concatenate([x_ref[q * 8 + i] for i in range(8)], axis=1)
        grad = dot(lhs, rhs)
        for i in range(8):
            o_ref[q * 8 + i] = grad[:, i * LANE : (i + 1) * LANE].T.astype(BF16)
        part = pl.ds(q * 8, 8)
        outs.append(begin(o_ref.at[part], out_ref.at[part], sem.at[q, 10]))
    for copy in outs:
        copy.wait()


def on_device(
    feats,
    ids,
    loss_mask,
    owner,
    shifts,
    target_gain,
    target_head,
    fc_weight,
    embed,
    draft_gain,
    layer_weight,
    draft_head,
):
    g = lax.axis_index("xh")
    c = lax.axis_index("c")
    y, xl, z = lax.axis_index("y"), lax.axis_index("xl"), lax.axis_index("z")
    pos = jnp.stack([g, c, z]).astype(jnp.int32)
    vocab_total = LANE * 128
    target_gain = target_gain.reshape(4, 16, LANE)
    draft_gain = draft_gain.reshape(4, 16, LANE)

    level = jnp.where(g == 0, feats[:, 0, :], feats[:, 2, :])
    column = spread(level, "z").reshape(8 * TOK, LANE)

    mid = feats[:, 1, :]
    rounds = (
        ((0, 1), (1, 0), (6, 7), (7, 6)),
        ((0, 2), (1, 3), (6, 4), (7, 5)),
        ((0, 3), (1, 2), (6, 5), (7, 4)),
    )
    r1, r2, r3 = [lax.ppermute(mid, ("xh", "y"), list(pairs)) for pairs in rounds]
    holder, even = (y // 2) == g, (y % 2) == 0
    near, far = jnp.where(holder, mid, r2), jnp.where(holder, r1, r3)
    pair = jnp.stack([jnp.where(even, near, far), jnp.where(even, far, near)])
    pair_got = swap(pair, "xl")
    quad = jnp.stack([jnp.where(xl == 0, pair, pair_got), jnp.where(xl == 0, pair_got, pair)])
    seq_ids = lax.dynamic_slice_in_dim(ids, c * TOK, TOK, 0)
    local_ids = seq_ids - g * embed.shape[0]
    inside = (local_ids >= 0) & (local_ids < embed.shape[0])
    picked = jnp.take(embed, jnp.clip(local_ids, 0, embed.shape[0] - 1), axis=0)
    picked = jnp.where(inside[:, None], picked, jnp.zeros((), BF16)).reshape(2, HALF, LANE)
    e_own = lax.dynamic_index_in_dim(picked, g, 0, keepdims=False)
    e_got = swap(lax.dynamic_index_in_dim(picked, 1 - g, 0, keepdims=False), "xh")

    column, quad, e_got = lax.optimization_barrier((column, quad, e_got))
    wide = spread(column, ("y", "xl")).reshape(64, TOK, LANE)
    up = [(i, (i + 1) % 8) for i in range(8)]
    down = [(i, (i + 7) % 8) for i in range(8)]
    ring, a, b = [quad], quad, quad
    for _ in range(3):
        a, b = lax.ppermute(a, "z", up), lax.ppermute(b, "z", down)
        ring += [a, b]
    ring += [lax.ppermute(a[0:1], "z", up), lax.ppermute(b[1:2], "z", down)]

    own_part, other_part = call(
        unite_kernel,
        (sds((HALF, LANE), F32), sds((HALF, LANE), F32)),
        (SMEM,) + (ANY,) * 11,
        flops=2 * 128 * 12288 * 128,
        nbytes=6 << 20,
        scratch=[
            pltpu.VMEM((64, TOK, LANE), BF16),
            pltpu.VMEM((8192, LANE), BF16),
            pltpu.VMEM((8, 2, 2, TOK, LANE), BF16),
            pltpu.VMEM((4096, LANE), BF16),
            pltpu.VMEM((TOK, LANE), F32),
        ],
        sems=18,
    )(pos, wide, *ring, fc_weight)
    part_got = swap(other_part, "xh")

    high, part_got = lax.optimization_barrier((wide, part_got))
    high_got = across_grp(high, ((3, 0), (2, 1)))

    state, e_rows, mix = call(
        first_kernel,
        (sds((HALF, LANE), F32), sds((HALF, LANE), BF16), sds((64, HALF, LANE), BF16)),
        (SMEM, VMEM, VMEM, VMEM, VMEM),
        big=False,
    )(shifts, own_part, part_got, e_own, e_got)

    rows64 = pltpu.VMEM((64, HALF, LANE), BF16)
    rows128 = pltpu.VMEM((64, TOK, LANE), BF16)
    weights = pltpu.VMEM((8192, LANE), BF16)
    tp = ("y", "xl", "z")
    mine, theirs, halves = [], [], []
    for step in range(2):
        rows = lax.all_to_all(mix, tp, 0, 0, tiled=True)
        if step == 1:
            t_logits = call(
                target_kernel,
                (sds((LANE, TOK), F32),),
                (SMEM, ANY, ANY, VMEM, ANY),
                flops=2 * 128 * 8192 * 128,
                nbytes=4 << 20,
                scratch=[rows128, weights, rows128],
                sems=5,
            )(pos, wide, high_got, target_gain, target_head)[0]
            rows, t_logits = lax.optimization_barrier((rows, t_logits))
        low, high, half, state, mix = call(
            functools.partial(layer_kernel, step),
            (
                sds((32, HALF, LANE), BF16),
                sds((32, HALF, LANE), BF16),
                sds((32, HALF, LANE), BF16),
                sds((HALF, LANE), F32),
                sds((64 if step == 0 else 8, HALF, LANE), BF16),
            ),
            (SMEM, SMEM, ANY, VMEM, ANY, VMEM, VMEM),
            flops=2 * 64 * 8192 * 128,
            nbytes=4 << 20,
            scratch=[rows64, weights, rows64],
            sems=8,
            far=(0, 1, 2),
        )(pos, shifts, rows, draft_gain, layer_weight, state, e_rows)
        mine.append((low, high))
        halves.append(half)
        theirs.append((across_grp(low), across_grp(high)))

    part = lax.all_to_all(mix, "z", 0, 0, tiled=True).reshape(8 * HALF, LANE)
    part, theirs[0], first_part = lax.optimization_barrier((part, theirs[0], theirs[1][0]))
    theirs[1] = (first_part, theirs[1][1])
    last = spread(part, ("xh", "y", "xl")).reshape(2, 64, HALF, LANE)

    early = [
        call(
            early_kernel,
            (sds((LANE, TOK), F32),),
            (SMEM,) + (ANY,) * 5,
            flops=2 * 128 * 8192 * 128,
            nbytes=4 << 20,
            scratch=[weights, rows64, rows64, pltpu.VMEM((TOK, LANE), F32)],
            sems=5,
        )(pos, draft_head, *mine[k], *theirs[k])[0]
        for k in range(2)
    ]
    n_last, half, l_last, targets, stat = call(
        logits_kernel,
        (
            sds((64, TOK, LANE), BF16),
            sds((32, TOK, LANE), BF16),
            sds((LANE, TOK), F32),
            sds((STEPS, LANE, TOK), F32),
            sds((8, 16, LANE), F32),
        ),
        (SMEM, SMEM, ANY, VMEM, ANY, VMEM, VMEM, VMEM),
        flops=2 * 128 * 8192 * 128,
        nbytes=6 << 20,
        scratch=[rows128, weights, rows128],
        sems=15,
        far=(0, 1),
    )(pos, shifts, last, draft_gain, draft_head, early[0], early[1], t_logits)

    across = [swap(v, "c") for v in (halves[0], *theirs[0], halves[1], *theirs[1], half)]

    stat = lax.all_to_all(stat, "z", 0, 0, tiled=True)
    stat = call(middle_kernel, (sds((16, 16, LANE), F32),), (VMEM,), big=False)(stat)[0]
    stat = lax.all_to_all(stat, ("xh", "y", "xl"), 0, 0, tiled=True)

    mask = lax.dynamic_slice_in_dim(loss_mask, c * TOK, TOK, 0).astype(F32)[None, :]
    grads, kl = call(
        functools.partial(grad_kernel, vocab_total),
        (sds((STEPS, LANE, TOK), BF16), sds((8, LANE), F32)),
        (SMEM,) + (VMEM,) * 6,
        big=False,
    )(pos, stat, mask, early[0], early[1], l_last, targets)
    grads_got, kl_got = swap(grads, "c"), swap(kl, "c")

    head_grad = call(
        head_kernel,
        (sds((32, LANE, LANE), BF16),),
        (SMEM, VMEM, VMEM) + (ANY,) * 16,
        flops=2 * 768 * 4096 * 128,
        nbytes=8 << 20,
        scratch=[pltpu.VMEM((32, 768, LANE), BF16), pltpu.VMEM((32, LANE, LANE), BF16)]
        + [pltpu.SemaphoreType.DMA((4, 11))],
        far=(0,),
    )(
        pos,
        grads,
        grads_got,
        *mine[0],
        *theirs[0],
        *mine[1],
        *theirs[1],
        n_last,
        *across,
    )[0].reshape(4096, LANE)

    blocks = TOK // BLK
    kl_own, kl_other = kl[:STEPS], kl_got[:STEPS]
    kl_all = jnp.where(c == 0, jnp.stack([kl_own, kl_other], 1), jnp.stack([kl_other, kl_own], 1))
    kl_all = kl_all.reshape(STEPS, 2, 1, blocks, BLK)
    hits = (owner[:, 0].reshape(2, blocks) == c).astype(jnp.int32)
    rank = jnp.cumsum(hits, axis=1) - 1
    pick = (hits[:, None, :] > 0) & (
        rank[:, None, :] == jnp.arange(MOST, dtype=jnp.int32)[None, :, None]
    )
    slot_kl = jnp.sum(jnp.where(pick[None, :, :, :, None], kl_all, 0.0), axis=3)
    return head_grad, slot_kl.reshape(STEPS, 2 * MOST * BLK)


def solution(mesh):
    fine = Mesh(np.asarray(mesh.devices).reshape(2, 4, 2, 8, 2), ("xh", "y", "xl", "z", "c"))
    tp = ("y", "xl", "z")
    every = ("xh",) + tp
    return jax.shard_map(
        on_device,
        mesh=fine,
        in_specs=(
            P("c", None, tp),
            P(),
            P(),
            P(),
            P(),
            P(),
            P(None, every),
            P("xh", tp),
            P("xh", tp),
            P(),
            P(None, tp),
            P(None, every),
        ),
        out_specs=(P("c", every), P(None, "c")),
        check_vma=False,
    )
```

```python
import functools

import jax
import jax.numpy as jnp
import numpy as np
from jax import lax
from jax.experimental import pallas as pl
from jax.experimental.pallas import tpu as pltpu
from jax.sharding import Mesh
from jax.sharding import PartitionSpec as P

BLK = 16
STEPS = 3
MOST = 6
LANE = 128
HALF = 64
TOK = 128
EPS = 1e-05

VMEM = pl.BlockSpec(memory_space=pltpu.VMEM)
SMEM = pl.BlockSpec(memory_space=pltpu.SMEM)
ANY = pl.BlockSpec(memory_space=pl.ANY)
F32 = jnp.float32
BF16 = jnp.bfloat16


def call(kernel, outs, ins, *, flops=0, nbytes=0, scratch=(), sems=0, far=(), big=True):
    return pl.pallas_call(
        kernel,
        out_shape=tuple(outs),
        in_specs=list(ins),
        out_specs=tuple(ANY if i in far else VMEM for i in range(len(outs))),
        scratch_shapes=list(scratch) + ([pltpu.SemaphoreType.DMA((sems,))] if sems else []),
        compiler_params=pltpu.CompilerParams(vmem_limit_bytes=(60 if big else 4) * 1024 * 1024),
        cost_estimate=pl.CostEstimate(flops=flops, bytes_accessed=nbytes, transcendentals=0),
    )


def sds(shape, dtype):
    return jax.ShapeDtypeStruct(shape, dtype)


def begin(source, target, sem):
    copy = pltpu.make_async_copy(source, target, sem)
    copy.start()
    return copy


def dot(a, b):
    return jnp.dot(a, b, preferred_element_type=F32)


def spread(values, axis):
    count = lax.axis_size(axis)
    return lax.all_to_all(
        jnp.broadcast_to(values[None], (count,) + values.shape), axis, 0, 0, tiled=True
    )


def across_grp(values, pairs=((0, 3), (1, 2), (2, 1), (3, 0))):
    return lax.ppermute(values, ("xh", "xl"), list(pairs))


def swap(values, axis):
    count = lax.axis_size(axis)
    return lax.ppermute(values, axis, [(i, (i + count // 2) % count) for i in range(count)])


def shift_lanes(values, shift):
    place = lax.broadcasted_iota(jnp.int32, values.shape, 1) & (BLK - 1)
    ahead = pltpu.roll(values, (TOK - shift) & (TOK - 1), 1)
    return jnp.where(place + shift < BLK, ahead, pltpu.roll(values, BLK - shift, 1))


def shift_rows(shift, rows):
    tok = lax.broadcasted_iota(jnp.int32, (rows, rows), 0)
    src = lax.broadcasted_iota(jnp.int32, (rows, rows), 1)
    want = (tok & ~(BLK - 1)) + ((tok & (BLK - 1)) + shift & (BLK - 1))
    return jnp.where(src == want, 1.0, 0.0).astype(BF16)


def unite_kernel(pos_ref, a_ref, *rest):
    ring, (fc_ref, own_ref, other_ref, x_ref, w_ref, m_ref, v_ref, acc_ref, sem) = rest[:9], rest[9:]
    g, z = pos_ref[0], pos_ref[2]
    whole = pl.multiple_of(g * 4096, 4096)
    middle = pl.multiple_of((1 - g) * 8192, 4096)
    first = []
    for i in range(4):
        rows = pl.ds(whole + i * 2048, 2048)
        first.append(begin(a_ref.at[pl.ds(i * 16, 16)], x_ref.at[pl.ds(i * 16, 16)], sem.at[2 * i]))
        first.append(begin(fc_ref.at[rows], w_ref.at[pl.ds(i * 2048, 2048)], sem.at[2 * i + 1]))
    second = [begin(fc_ref.at[pl.ds(middle, 4096)], v_ref, sem.at[8])]
    for n, (ref, away) in enumerate(zip(ring[:7], (0, -1, 1, -2, 2, -3, 3))):
        second.append(begin(ref, m_ref.at[(z + away + 8) & 7], sem.at[9 + n]))
    second.append(begin(ring[7], m_ref.at[(z + 4) & 7, pl.ds(0, 1)], sem.at[16]))
    second.append(begin(ring[8], m_ref.at[(z + 4) & 7, pl.ds(1, 1)], sem.at[17]))
    acc = jnp.zeros((TOK, LANE), F32)
    for i in range(4):
        first[2 * i].wait()
        first[2 * i + 1].wait()
        lhs = jnp.concatenate([x_ref[i * 16 + j] for j in range(16)], axis=1)
        acc += dot(lhs, w_ref[i * 2048 : (i + 1) * 2048, :])
    for copy in second:
        copy.wait()
    for yl in range(2):
        for xl in range(2):
            lhs = jnp.concatenate([m_ref[j, xl, yl] for j in range(8)], axis=1)
            at = (yl * 2 + xl) * 1024
            acc += dot(lhs, v_ref[at : at + 1024, :])
    acc_ref[...] = acc
    own_ref[...] = acc_ref[pl.ds(pl.multiple_of(g * HALF, HALF), HALF), :]
    other_ref[...] = acc_ref[pl.ds(pl.multiple_of((1 - g) * HALF, HALF), HALF), :]


def first_state(own_ref, got_ref, e_own_ref, e_got_ref):
    state = (own_ref[...] + got_ref[...]).astype(BF16).astype(F32)
    return state, (e_own_ref[...].astype(F32) + e_got_ref[...].astype(F32)).astype(BF16)


def first_kernel(shifts_ref, own_ref, got_ref, e_own_ref, e_got_ref, mix_ref):
    state, rows = first_state(own_ref, got_ref, e_own_ref, e_got_ref)
    mixed = (state + dot(shift_rows(shifts_ref[0], HALF), rows)).astype(BF16)
    for i in range(64):
        mix_ref[i] = mixed


def normalize_into(x_of, gain_ref, count, rows, out_of, ready=None):
    total = jnp.zeros((rows, LANE), F32)
    for p in range(count):
        if ready is not None and p % 16 == 0:
            for copy in ready[p // 16]:
                copy.wait()
        v = x_of(p).astype(F32)
        total += v * v
    scale = lax.rsqrt(jnp.sum(total, axis=1, keepdims=True) / (count * LANE) + EPS)
    for i in range(count // 16):
        gain = gain_ref[i].astype(F32)
        for j in range(16):
            p = i * 16 + j
            out_of(p, (x_of(p).astype(F32) * scale * gain[j : j + 1, :]).astype(BF16))


def row_dot(n_of, w_ref, rows):
    acc = jnp.zeros((rows, LANE), F32)
    for i in range(4):
        lhs = jnp.concatenate([n_of(i * 16 + j) for j in range(16)], axis=1)
        acc += dot(lhs, w_ref[i * 2048 : (i + 1) * 2048, :])
    return acc


def layer_kernel(step, shifts_ref, far_x_ref, gain_ref, far_w_ref, *rest):
    if step == 0:
        parts, (low_ref, high_ref, next_ref, e_ref, mix_ref, x_ref, w_ref, n_ref, sem) = rest[:4], rest[4:]
    else:
        state_ref, e_ref, low_ref, high_ref, mix_ref, x_ref, w_ref, n_ref, sem = rest
    ready = []
    for i in range(4):
        part = pl.ds(i * 16, 16)
        ready.append([begin(far_x_ref.at[part], x_ref.at[part], sem.at[i])])
    weights = begin(far_w_ref, w_ref, sem.at[4])

    def put(p, value):
        n_ref[p] = value

    normalize_into(lambda p: x_ref[p], gain_ref, 64, HALF, put, ready)
    low = begin(n_ref.at[pl.ds(0, 32)], low_ref, sem.at[5])
    high = begin(n_ref.at[pl.ds(32, 32)], high_ref, sem.at[6])
    if step == 0:
        state, rows = first_state(*parts)
        e_ref[...] = rows
    else:
        state, rows = state_ref[...], e_ref[...]
    weights.wait()
    acc = row_dot(lambda p: n_ref[p], w_ref, HALF)
    state = state + acc * jax.nn.sigmoid(acc)
    mixed = (state + dot(shift_rows(shifts_ref[step + 1], HALF), rows)).astype(BF16)
    if step == 0:
        next_ref[...] = state
        for i in range(64):
            mix_ref[i] = mixed
    else:
        for i in range(8):
            mix_ref[i] = mixed
    low.wait()
    high.wait()


def target_kernel(
    pos_ref, own_ref, got_ref, gain_ref, far_w_ref, logits_ref, x_ref, w_ref, n_ref, sem
):
    weights = begin(far_w_ref, w_ref, sem.at[4])
    here = pos_ref[0]
    for source, which in ((got_ref, 0), (own_ref, 1)):

        @pl.when(here == which)
        def _(source=source):
            for i in range(4):
                part = pl.ds(i * 16, 16)
                begin(source.at[part], x_ref.at[part], sem.at[i])

    ready = []
    for i in range(4):
        part = pl.ds(i * 16, 16)
        ready.append([pltpu.make_async_copy(own_ref.at[part], x_ref.at[part], sem.at[i])])

    def put(p, value):
        n_ref[p] = value

    normalize_into(lambda p: x_ref[p], gain_ref, 64, TOK, put, ready)
    weights.wait()
    logits = row_dot(lambda p: n_ref[p], w_ref, TOK).T
    logits_ref[...] = logits


def early_kernel(
    pos_ref, far_w_ref, a_low_ref, a_high_ref, b_low_ref, b_high_ref, l_ref, w_ref, a_ref, b_ref, rows_ref, sem
):
    low, high = pl.ds(0, 32), pl.ds(32, 32)
    copies = [
        begin(far_w_ref, w_ref, sem.at[0]),
        begin(a_low_ref, a_ref.at[low], sem.at[1]),
        begin(a_high_ref, a_ref.at[high], sem.at[2]),
        begin(b_low_ref, b_ref.at[low], sem.at[3]),
        begin(b_high_ref, b_ref.at[high], sem.at[4]),
    ]
    g = pos_ref[0]
    acc = jnp.zeros((TOK, LANE), F32)
    for i in range(4):
        for n in ((0, 1, 3), (), (2, 4), ())[i]:
            copies[n].wait()
        group = range(i * 16, i * 16 + 16)
        lhs = jnp.concatenate(
            [jnp.concatenate([ref[p] for p in group], axis=1) for ref in (a_ref, b_ref)], axis=0
        )
        acc += dot(lhs, w_ref[i * 2048 : (i + 1) * 2048, :])
    rows_ref[pl.ds(pl.multiple_of(g * HALF, HALF), HALF), :] = acc[:HALF]
    rows_ref[pl.ds(pl.multiple_of((1 - g) * HALF, HALF), HALF), :] = acc[HALF:]
    l_ref[...] = rows_ref[...].T


def logits_kernel(pos_ref, shifts_ref, far_x_ref, gain_ref, far_w_ref, l0_ref, t_ref, *rest):
    far, (low_ref, high_ref, l1_ref, l_ref, tk_ref, stat_ref, x_ref, w_ref, n_ref, r_ref, sem) = (
        rest[:4],
        rest[4:],
    )
    ready = []
    for i in range(4):
        part = pl.ds(i * 16, 16)
        pair = []
        for h in range(2):
            rows = pl.ds(h * HALF, HALF)
            pair.append(begin(far_x_ref.at[h, part], x_ref.at[part, rows], sem.at[7 + 2 * i + h]))
        ready.append(pair)
    weights = begin(far_w_ref, w_ref, sem.at[4])
    second = []
    for n, ref in enumerate(far):
        target = r_ref.at[pl.ds(n % 2 * 32, 32), pl.ds(n // 2 * HALF, HALF)]
        second.append(begin(ref, target, sem.at[15 + n]))

    def put(p, value):
        n_ref[p] = value

    normalize_into(lambda p: x_ref[p], gain_ref, 64, TOK, put, ready)
    low = begin(n_ref.at[pl.ds(0, 32)], low_ref, sem.at[5])
    high = begin(n_ref.at[pl.ds(32, 32)], high_ref, sem.at[6])
    for copy in [weights] + second:
        copy.wait()
    acc = jnp.zeros((2 * TOK, LANE), F32)
    for i in range(4):
        group = range(i * 16, i * 16 + 16)
        lhs = jnp.concatenate(
            [jnp.concatenate([ref[p] for p in group], axis=1) for ref in (n_ref, r_ref)], axis=0
        )
        acc += dot(lhs, w_ref[i * 2048 : (i + 1) * 2048, :])
    l_ref[...] = acc[:TOK].T
    l1_ref[...] = pltpu.roll(acc[TOK:].T, pos_ref[0] * HALF, 1)
    stats = []
    for k, ref in enumerate((l0_ref, l1_ref, l_ref)):
        logits, wanted = ref[...], shift_lanes(t_ref[...], shifts_ref[k])
        tk_ref[k] = wanted
        peak = jnp.max(logits, axis=0, keepdims=True)
        top = jnp.max(wanted, axis=0, keepdims=True)
        logits, wanted = logits - peak, wanted - top
        target = jnp.exp(wanted)
        total = jnp.sum(jnp.exp(logits), axis=0, keepdims=True)
        mass = jnp.sum(target, axis=0, keepdims=True)
        cross = jnp.sum(target * (wanted - logits), axis=0, keepdims=True)
        stats += [peak, total, top, mass, cross]
    rows = jnp.concatenate(stats + [jnp.zeros((1, LANE), F32)], axis=0)
    for i in range(8):
        stat_ref[i] = rows
    low.wait()
    high.wait()


def combine(blocks):
    rows = []
    for k in range(STEPS):
        peaks, totals, tops, masses, crosses = [blocks[:, 5 * k + i, :] for i in range(5)]
        peak = jnp.max(peaks, axis=0, keepdims=True)
        top = jnp.max(tops, axis=0, keepdims=True)
        total = jnp.sum(totals * jnp.exp(peaks - peak), axis=0, keepdims=True)
        share = jnp.exp(tops - top)
        mass = jnp.sum(masses * share, axis=0, keepdims=True)
        moved = crosses + masses * ((tops - top) - (peaks - peak))
        cross = jnp.sum(moved * share, axis=0, keepdims=True)
        rows.append((peak, total, top, mass, cross))
    return rows


def middle_kernel(in_ref, out_ref):
    rows = []
    for item in combine(in_ref[...]):
        rows += list(item)
    rows = jnp.concatenate(rows + [jnp.zeros((1, LANE), F32)], axis=0)
    for i in range(16):
        out_ref[i] = rows


def grad_kernel(vocab_total, pos_ref, in_ref, mask_ref, *rest):
    l_refs, (tk_ref, grad_ref, kl_ref) = rest[:3], rest[3:]
    g = pos_ref[0]
    mask = mask_ref[...]
    weight = mask * (vocab_total / (STEPS * BLK))
    scores = []
    for k, (peak, total, top, mass, cross) in enumerate(combine(in_ref[...])):
        soft = jnp.exp(l_refs[k][...] - peak) / total
        target = (jnp.exp(tk_ref[k] - top) / mass).astype(BF16).astype(F32)
        grad = weight * (soft - target)
        if k < 2:
            grad = pltpu.roll(grad, g * HALF, 1)
        grad_ref[k] = grad.astype(BF16)
        scores.append((cross / mass - jnp.log(mass) + jnp.log(total)) * mask)
    kl_ref[...] = jnp.concatenate(scores + [jnp.zeros((5, LANE), F32)], axis=0)


def head_kernel(pos_ref, g_ref, h_ref, *rest):
    far, (out_ref, x_ref, o_ref, sem) = rest[:20], rest[20:]
    core = pos_ref[1]

    def copies_of(q, which):
        at, copies = 0, []
        for n in range(10):
            ref = far[2 * n + which]
            count = ref.shape[1]
            start = q * 8
            target = x_ref.at[pl.ds(q * 8, 8), pl.ds(at, count)]
            copies.append(pltpu.make_async_copy(ref.at[pl.ds(start, 8)], target, sem.at[q, n]))
            at += count
        return copies

    for which in range(2):

        @pl.when(core == which)
        def _(which=which):
            for q in range(4):
                for copy in copies_of(q, which):
                    copy.start()

    copies = [copies_of(q, 0) for q in range(4)]
    lhs = jnp.concatenate(
        [g_ref[0], g_ref[1], g_ref[2], h_ref[0], h_ref[1], h_ref[2]], axis=1
    )
    outs = []
    for q in range(4):
        for copy in copies[q]:
            copy.wait()
        rhs = jnp.concatenate([x_ref[q * 8 + i] for i in range(8)], axis=1)
        grad = dot(lhs, rhs)
        for i in range(8):
            o_ref[q * 8 + i] = grad[:, i * LANE : (i + 1) * LANE].T.astype(BF16)
        part = pl.ds(q * 8, 8)
        outs.append(begin(o_ref.at[part], out_ref.at[part], sem.at[q, 10]))
    for copy in outs:
        copy.wait()


def on_device(
    feats,
    ids,
    loss_mask,
    owner,
    shifts,
    target_gain,
    target_head,
    fc_weight,
    embed,
    draft_gain,
    layer_weight,
    draft_head,
):
    g = lax.axis_index("xh")
    c = lax.axis_index("c")
    y, xl, z = lax.axis_index("y"), lax.axis_index("xl"), lax.axis_index("z")
    pos = jnp.stack([g, c, z]).astype(jnp.int32)
    vocab_total = LANE * 128
    target_gain = target_gain.reshape(4, 16, LANE)
    draft_gain = draft_gain.reshape(4, 16, LANE)

    level = jnp.where(g == 0, feats[:, 0, :], feats[:, 2, :])
    column = spread(level, "z").reshape(8 * TOK, LANE)

    mid = feats[:, 1, :]
    rounds = (
        ((0, 1), (1, 0), (6, 7), (7, 6)),
        ((0, 2), (1, 3), (6, 4), (7, 5)),
        ((0, 3), (1, 2), (6, 5), (7, 4)),
    )
    r1, r2, r3 = [lax.ppermute(mid, ("xh", "y"), list(pairs)) for pairs in rounds]
    holder, even = (y // 2) == g, (y % 2) == 0
    near, far = jnp.where(holder, mid, r2), jnp.where(holder, r1, r3)
    pair = jnp.stack([jnp.where(even, near, far), jnp.where(even, far, near)])
    pair_got = swap(pair, "xl")
    quad = jnp.stack([jnp.where(xl == 0, pair, pair_got), jnp.where(xl == 0, pair_got, pair)])
    seq_ids = lax.dynamic_slice_in_dim(ids, c * TOK, TOK, 0)
    local_ids = seq_ids - g * embed.shape[0]
    inside = (local_ids >= 0) & (local_ids < embed.shape[0])
    picked = jnp.take(embed, jnp.clip(local_ids, 0, embed.shape[0] - 1), axis=0)
    picked = jnp.where(inside[:, None], picked, jnp.zeros((), BF16)).reshape(2, HALF, LANE)
    e_own = lax.dynamic_index_in_dim(picked, g, 0, keepdims=False)
    e_got = swap(lax.dynamic_index_in_dim(picked, 1 - g, 0, keepdims=False), "xh")

    column, quad, e_got = lax.optimization_barrier((column, quad, e_got))
    wide = spread(column, ("y", "xl")).reshape(64, TOK, LANE)
    up = [(i, (i + 1) % 8) for i in range(8)]
    down = [(i, (i + 7) % 8) for i in range(8)]
    ring, a, b = [quad], quad, quad
    for _ in range(3):
        a, b = lax.ppermute(a, "z", up), lax.ppermute(b, "z", down)
        ring += [a, b]
    ring += [lax.ppermute(a[0:1], "z", up), lax.ppermute(b[1:2], "z", down)]

    own_part, other_part = call(
        unite_kernel,
        (sds((HALF, LANE), F32), sds((HALF, LANE), F32)),
        (SMEM,) + (ANY,) * 11,
        flops=2 * 128 * 12288 * 128,
        nbytes=6 << 20,
        scratch=[
            pltpu.VMEM((64, TOK, LANE), BF16),
            pltpu.VMEM((8192, LANE), BF16),
            pltpu.VMEM((8, 2, 2, TOK, LANE), BF16),
            pltpu.VMEM((4096, LANE), BF16),
            pltpu.VMEM((TOK, LANE), F32),
        ],
        sems=18,
    )(pos, wide, *ring, fc_weight)
    part_got = swap(other_part, "xh")

    high, part_got = lax.optimization_barrier((wide, part_got))
    high_got = across_grp(high, ((3, 0), (2, 1)))

    mix = call(
        first_kernel,
        (sds((64, HALF, LANE), BF16),),
        (SMEM, VMEM, VMEM, VMEM, VMEM),
        big=False,
    )(shifts, own_part, part_got, e_own, e_got)[0]

    rows64 = pltpu.VMEM((64, HALF, LANE), BF16)
    rows128 = pltpu.VMEM((64, TOK, LANE), BF16)
    weights = pltpu.VMEM((8192, LANE), BF16)
    tp = ("y", "xl", "z")
    mine, theirs = [], []
    for step in range(2):
        rows = lax.all_to_all(mix, tp, 0, 0, tiled=True)
        if step == 1:
            rows, high_got = lax.optimization_barrier((rows, high_got))
        held = (own_part, part_got, e_own, e_got) if step == 0 else (state, e_rows)
        rows32 = sds((32, HALF, LANE), BF16)
        kept = (sds((HALF, LANE), F32), sds((HALF, LANE), BF16)) if step == 0 else ()
        low, high, *kept, mix = call(
            functools.partial(layer_kernel, step),
            (rows32, rows32, *kept, sds((64 if step == 0 else 8, HALF, LANE), BF16)),
            (SMEM, ANY, VMEM, ANY) + (VMEM,) * len(held),
            flops=2 * 64 * 8192 * 128,
            nbytes=4 << 20,
            scratch=[rows64, weights, rows64],
            sems=7,
            far=(0, 1),
        )(shifts, rows, draft_gain, layer_weight, *held)
        if step == 0:
            state, e_rows = kept
        mine.append((low, high))
        theirs.append((across_grp(low), across_grp(high)))

    part = lax.all_to_all(mix, "z", 0, 0, tiled=True).reshape(8 * HALF, LANE)
    t_logits = call(
        target_kernel,
        (sds((LANE, TOK), F32),),
        (SMEM, ANY, ANY, VMEM, ANY),
        flops=2 * 128 * 8192 * 128,
        nbytes=4 << 20,
        scratch=[rows128, weights, rows128],
        sems=5,
    )(pos, wide, high_got, target_gain, target_head)[0]
    first_low, t_logits = lax.optimization_barrier((theirs[0][0], t_logits))
    theirs[0] = (first_low, theirs[0][1])
    l_first = call(
        early_kernel,
        (sds((LANE, TOK), F32),),
        (SMEM,) + (ANY,) * 5,
        flops=2 * 128 * 8192 * 128,
        nbytes=4 << 20,
        scratch=[weights, rows64, rows64, pltpu.VMEM((TOK, LANE), F32)],
        sems=5,
    )(pos, draft_head, *mine[0], *theirs[0])[0]
    part, low, t_logits, l_first = lax.optimization_barrier(
        (part, theirs[1][0], t_logits, l_first)
    )
    theirs[1] = (low, theirs[1][1])
    last = spread(part, ("xh", "y", "xl")).reshape(2, 64, HALF, LANE)

    n_low, n_high, l_second, l_last, targets, stat = call(
        logits_kernel,
        (
            sds((32, TOK, LANE), BF16),
            sds((32, TOK, LANE), BF16),
            sds((LANE, TOK), F32),
            sds((LANE, TOK), F32),
            sds((STEPS, LANE, TOK), F32),
            sds((8, 16, LANE), F32),
        ),
        (SMEM, SMEM, ANY, VMEM, ANY, VMEM, VMEM) + (ANY,) * 4,
        flops=2 * 128 * 8192 * 128,
        nbytes=6 << 20,
        scratch=[rows128, weights, rows128, rows128],
        sems=19,
        far=(0, 1),
    )(pos, shifts, last, draft_gain, draft_head, l_first, t_logits, *mine[1], *theirs[1])

    rows = [v for k in range(2) for v in (*mine[k], *theirs[k])]
    across = [swap(v, "c") for v in rows]
    n_across = [swap(v, "c") for v in (n_low, n_high)]

    stat = lax.all_to_all(stat, "z", 0, 0, tiled=True)
    stat, across = lax.optimization_barrier((stat, across))
    stat = call(middle_kernel, (sds((16, 16, LANE), F32),), (VMEM,), big=False)(stat)[0]
    stat = lax.all_to_all(stat, ("xh", "y", "xl"), 0, 0, tiled=True)
    stat, n_across = lax.optimization_barrier((stat, n_across))

    mask = lax.dynamic_slice_in_dim(loss_mask, c * TOK, TOK, 0).astype(F32)[None, :]
    grads, kl = call(
        functools.partial(grad_kernel, vocab_total),
        (sds((STEPS, LANE, TOK), BF16), sds((8, LANE), F32)),
        (SMEM,) + (VMEM,) * 6,
        big=False,
    )(pos, stat, mask, l_first, l_second, l_last, targets)
    grads_got, kl_got = swap(grads, "c"), swap(kl, "c")

    head_grad = call(
        head_kernel,
        (sds((32, LANE, LANE), BF16),),
        (SMEM, VMEM, VMEM) + (ANY,) * 20,
        flops=2 * 768 * 4096 * 128,
        nbytes=8 << 20,
        scratch=[pltpu.VMEM((32, 768, LANE), BF16), pltpu.VMEM((32, LANE, LANE), BF16)]
        + [pltpu.SemaphoreType.DMA((4, 11))],
        far=(0,),
    )(
        pos,
        grads,
        grads_got,
        *rows,
        n_low,
        n_high,
        *across,
        *n_across,
    )[0].reshape(4096, LANE)

    blocks = TOK // BLK
    kl_own, kl_other = kl[:STEPS], kl_got[:STEPS]
    kl_all = jnp.where(c == 0, jnp.stack([kl_own, kl_other], 1), jnp.stack([kl_other, kl_own], 1))
    kl_all = kl_all.reshape(STEPS, 2, 1, blocks, BLK)
    hits = (owner[:, 0].reshape(2, blocks) == c).astype(jnp.int32)
    rank = jnp.cumsum(hits, axis=1) - 1
    pick = (hits[:, None, :] > 0) & (
        rank[:, None, :] == jnp.arange(MOST, dtype=jnp.int32)[None, :, None]
    )
    slot_kl = jnp.sum(jnp.where(pick[None, :, :, :, None], kl_all, 0.0), axis=3)
    return head_grad, slot_kl.reshape(STEPS, 2 * MOST * BLK)


def solution(mesh):
    fine = Mesh(np.asarray(mesh.devices).reshape(2, 4, 2, 8, 2), ("xh", "y", "xl", "z", "c"))
    tp = ("y", "xl", "z")
    every = ("xh",) + tp
    return jax.shard_map(
        on_device,
        mesh=fine,
        in_specs=(
            P("c", None, tp),
            P(),
            P(),
            P(),
            P(),
            P(),
            P(None, every),
            P("xh", tp),
            P("xh", tp),
            P(),
            P(None, tp),
            P(None, every),
        ),
        out_specs=(P("c", every), P(None, "c")),
        check_vma=False,
    )
```
